1024 devices in a mesh: dp: 64 (over x_lo, z), tensor: 16 (over x_hi, y, core).
Axes of the slice: x: 4 (x_hi: 2, x_lo: 2; x = x_hi * 2 + x_lo), y: 4, z: 32, core: 2. Of those that a mesh axis runs over, the one named last changes fastest.
Arguments:
- activations: bfloat16 [8192, 6144], P('dp'), may hold values from -3 to 3
- grad_hidden: bfloat16 [8192, 24576], P('dp', 'tensor'), may hold values from -0.59765625 to 0.59765625
- weight_tiles: bfloat16 [16, 64, 128, 128], P('tensor'), may hold values from -0.5 to 0.5
- tile_slots: int32 [16, 64], P('tensor'), may hold values from 0 to 575, as said below
- owner_map: int32 [16, 64], P('tensor'), may hold values from 0 to 63, as said below
Outputs:
- grad_input: float32 [8192, 6144], P('dp', 'tensor')
- grad_weight: float32 [64, 2048, 128], P('dp', 'tensor')
The draws below stay inside these ranges and needn't reach their ends.
Inputs may be any that keep to these rules, and one draw needn't show every extreme that they name: `tile_slots`: each row holds 64 distinct positions in increasing order, the first being 0 and the last the largest position. `owner_map`: in each row every owner is named by exactly 1 entry.
All inputs are finite; a program needn't handle non-finite values.
Results may differ from the reference program's by a relative error of at most 0.0029.
Values sent between devices are 32-bit elements; how exact they have to be, the bound alone decides.
No kernel may reach another device: no remote copies, remote signals or barrier semaphores. Data moves between devices by JAX's collectives and lax.ppermute only.
A program may use at most 64 MiB of HBM per device.

```python
import jax
import jax.numpy as jnp
from jax import lax

D = 6144
FF = 24576
TILE = 128
OWN = 1
TOKENS = 8192
NT = 64
N_DP = 64
N_TENSOR = 16


def draw_tile_slots(key, part):
    key = jax.random.fold_in(key, 11)
    position_count = D // TILE * (FF // N_TENSOR // TILE)
    tile_count = OWN * N_DP

    def draw_row(subkey):
        shuffled = jax.random.permutation(subkey, position_count - 2).astype(jnp.int32) + 1
        chosen = jnp.concatenate([jnp.zeros((1,), jnp.int32), shuffled[:tile_count - 2], jnp.full((1,), position_count - 1, jnp.int32)])
        return jnp.sort(chosen)
    return jax.vmap(draw_row)(jax.random.split(key, N_TENSOR))


def draw_owner_map(key, part):
    key = jax.random.fold_in(key, 23)
    tile_count = OWN * N_DP

    def draw_row(subkey):
        return (jax.random.permutation(subkey, tile_count).astype(jnp.int32) // OWN).astype(jnp.int32)
    return jax.vmap(draw_row)(jax.random.split(key, N_TENSOR))


def level_of(key, shape, cuts, low, high):
    gain, own = 1.0, jax.random.fold_in(key, 6)
    for dim, parts in cuts:
        steps = jnp.exp(jax.random.uniform(jax.random.fold_in(own, dim), (parts,), jnp.float32, low / len(cuts), high / len(cuts)))
        gain = gain * jnp.repeat(steps, shape[dim] // parts).reshape([-1 if axis == dim else 1 for axis in range(len(shape))])
    return gain


def scatter_about(key, dims, spread, limit, shards=(), kind=jnp.bfloat16):
    values = jax.random.normal(key, dims, jnp.float32) * spread
    if len(shards) > 0:
        values = level_of(key, dims, shards, -0.22, 0.18) * values
    return jnp.clip(values, min=-limit, max=limit).astype(kind)


def setup_inputs(seed: int = 0) -> dict:
    streams_of = jax.random.split(jax.random.key(seed), 6)
    return {
        "activations": scatter_about(streams_of[0], (TOKENS, D), 0.5, 3.0, ((0, 64),)),
        "grad_hidden": scatter_about(streams_of[1], (TOKENS, FF), 0.1, 0.59765625, ((0, 64), (1, 16))),
        "weight_tiles": scatter_about(streams_of[2], (N_TENSOR, NT, TILE, TILE), TILE ** -0.5, 0.5, ((0, 16),)),
        "tile_slots": draw_tile_slots(jax.random.fold_in(streams_of[5], 71), 0),
        "owner_map": draw_owner_map(jax.random.fold_in(streams_of[5], 71), 0),
    }


root_two_pi = 0.7978845608028654
cubic_term = 0.044715


def gelu_slope(preact):
    inner = root_two_pi * (preact + cubic_term * preact * preact * preact)
    tangent = jnp.tanh(inner)
    return 0.5 * (1.0 + tangent) + 0.5 * preact * (1.0 - tangent * tangent) * root_two_pi * (1.0 + 3.0 * cubic_term * preact * preact)


def reference(activations, grad_hidden, weight_tiles, tile_slots, owner_map):
    tokens = activations.shape[0]
    local_width = FF // N_TENSOR
    col_panels = local_width // TILE
    row_panels = D // TILE
    x_blocks = activations.reshape(tokens, row_panels, TILE)
    grad_parts = grad_hidden.reshape(tokens, N_TENSOR, local_width).transpose(1, 0, 2)

    def per_share(inputs):
        tiles, positions, owners, grad_part = inputs
        row_index = (positions // col_panels).astype(jnp.int32)
        col_index = (positions % col_panels).astype(jnp.int32)
        x_sel = jnp.take(x_blocks, row_index, axis=1).astype(jnp.float32)
        tiles_wide = tiles.astype(jnp.float32)
        pieces = jnp.einsum('tnk,nkj->ntj', x_sel, tiles_wide, precision=lax.Precision.HIGHEST)
        col_onehot = (col_index[:, None] == jnp.arange(col_panels, dtype=jnp.int32)[None, :]).astype(jnp.float32)
        row_onehot = (row_index[:, None] == jnp.arange(row_panels, dtype=jnp.int32)[None, :]).astype(jnp.float32)
        preact = jnp.einsum('nc,ntj->tcj', col_onehot, pieces, precision=lax.Precision.HIGHEST).reshape(tokens, local_width)
        grad_pre = (grad_part.astype(jnp.float32) * gelu_slope(preact)).astype(jnp.bfloat16)
        g_sel = jnp.take(grad_pre.reshape(tokens, col_panels, TILE), col_index, axis=1).astype(jnp.float32)
        back_rows = jnp.einsum('tnj,nkj->ntk', g_sel, tiles_wide, precision=lax.Precision.HIGHEST)
        input_part = jnp.einsum('nr,ntk->trk', row_onehot, back_rows, precision=lax.Precision.HIGHEST).reshape(tokens, D)
        weight_grad = jnp.einsum('tnk,tnj->nkj', x_sel, g_sel, precision=lax.Precision.HIGHEST)
        owner_order = jnp.argsort(owners, stable=True).astype(jnp.int32)
        return input_part, jnp.take(weight_grad, owner_order, axis=0)

    input_parts, grouped = lax.map(per_share, (weight_tiles, tile_slots, owner_map, grad_parts))
    grad_input = jnp.sum(input_parts, axis=0)
    grad_weight = grouped.transpose(1, 0, 2, 3).reshape(N_DP * OWN, N_TENSOR * TILE, TILE)
    return grad_input, grad_weight
```

```python
import functools

import jax
import jax.numpy as jnp
from jax import lax
from jax.experimental import pallas as pl
from jax.experimental.pallas import tpu as pltpu
from jax.sharding import PartitionSpec as P

TILE = 128
GROUP = 4
X_ROWS, X_UP = 48, 24
Z_ROWS, Z_UP = 80, 40
X_LO, X_HI, CORES = 2, 2, 2
RING = 4

root_two_pi = 0.7978845608028654
cubic_term = 0.044715


def gelu_slope(preact):
    inner = root_two_pi * (preact + cubic_term * preact * preact * preact)
    tangent = jnp.tanh(inner)
    return 0.5 * (1.0 + tangent) + 0.5 * preact * (1.0 - tangent * tangent) * root_two_pi * (
        1.0 + 3.0 * cubic_term * preact * preact
    )


def panel(index):
    return pl.ds(pl.multiple_of(index * TILE, TILE), TILE)


def weight_kernel(n_tiles, n_cols, slots, places, x_ref, g_ref, tiles_ref, gp_ref, xf_ref, up_ref, down_ref, pre_ref):
    pre_ref[...] = jnp.zeros_like(pre_ref)

    def project(step, carry):
        parts = []
        for k in range(GROUP):
            i = step * GROUP + k
            slot = slots[0, i]
            parts.append((slot % n_cols, jnp.dot(
                x_ref[:, panel(slot // n_cols)], tiles_ref[i], preferred_element_type=jnp.float32
            )))
        for col, part in parts:
            pre_ref[col] += part
        return carry

    lax.fori_loop(0, n_tiles // GROUP, project, 0)
    for col in range(n_cols):
        grad = g_ref[:, col * TILE:(col + 1) * TILE].astype(jnp.float32)
        gp_ref[col] = (grad * gelu_slope(pre_ref[col])).astype(jnp.bfloat16)

    def weight_grad(step, carry):
        for k in range(GROUP):
            i = step * GROUP + k
            slot = slots[0, i]
            part = lax.dot_general(
                x_ref[:, panel(slot // n_cols)], gp_ref[slot % n_cols],
                (((0,), (0,)), ((), ())), preferred_element_type=jnp.float32,
            )
            xf_ref[places[0, i]] = part[:X_ROWS]
            up_ref[places[1, i]] = part[X_ROWS:X_ROWS + Z_UP]
            down_ref[places[1, i]] = part[X_ROWS + Z_UP:]
        return carry

    lax.fori_loop(0, n_tiles // GROUP, weight_grad, 0)


def input_kernel(n_tiles, n_cols, slots, spots, gp_ref, tiles_ref, gi_ref):
    gi_ref[...] = jnp.zeros_like(gi_ref)

    def back(step, carry):
        parts = []
        for k in range(GROUP):
            i = step * GROUP + k
            parts.append((spots[0, i], lax.dot_general(
                gp_ref[slots[0, i] % n_cols], tiles_ref[i],
                (((1,), (1,)), ((), ())), preferred_element_type=jnp.float32,
            )))
        for spot, part in parts:
            gi_ref[spot] += part
        return carry

    lax.fori_loop(0, n_tiles // GROUP, back, 0)


def z_pairs(z_len, stride, way):
    step = [stride if (z // stride) % 2 == 0 else -stride for z in range(z_len)]
    return [(z, (z + way * step[z]) % z_len) for z in range(z_len)]


def along_z(value, z_len, pairs):
    return lax.ppermute(value, "dp", [(x * z_len + a, x * z_len + b) for x in range(X_LO) for a, b in pairs])


def swap_x(value, z_len):
    n = X_LO * z_len
    return lax.ppermute(value, "dp", [(i, (i + z_len) % n) for i in range(n)])


def halve(up, down, z_len, z, stride):
    digit = (z // stride) % 2
    half = up.shape[0] // 2
    pick = lambda value, which: lax.dynamic_slice_in_dim(value, which * half, half, 0)
    got_up = along_z(pick(up, 1 - digit), z_len, z_pairs(z_len, stride, 1))
    got_down = along_z(pick(down, 1 - digit), z_len, z_pairs(z_len, stride, -1))
    return pick(up, digit) + got_up, pick(down, digit) + got_down


def reduce_weight(xf, up, down, z_len):
    z = lax.axis_index("dp") % z_len
    n = xf.shape[0] // 4
    first_up, first_down = z_pairs(z_len, 1, 1), z_pairs(z_len, 1, -1)
    got_x = swap_x(xf[2 * n:], z_len)
    got_up = along_z(up[2 * n:], z_len, first_up)
    got_down = along_z(down[2 * n:], z_len, first_down)
    send = got_x[n:] + xf[n:2 * n]
    got_xu = along_z(send[:, :X_UP], z_len, first_up)
    got_xd = along_z(send[:, X_UP:], z_len, first_down)
    got_z = swap_x(jnp.concatenate([got_up[n:] + up[n:2 * n], got_down[n:] + down[n:2 * n]], axis=1), z_len)
    keep = got_x[:n] + xf[:n]
    up_now = jnp.concatenate([keep[:, :X_UP] + got_xu, got_up[:n] + up[:n] + got_z[:, :Z_UP]], axis=1)
    down_now = jnp.concatenate([keep[:, X_UP:] + got_xd, got_down[:n] + down[:n] + got_z[:, Z_UP:]], axis=1)
    stride = 2
    while up_now.shape[0] > RING:
        up_now, down_now = halve(up_now, down_now, z_len, z, stride)
        stride *= 2
    mine = z // stride
    chunk = lambda value, k: lax.dynamic_slice_in_dim(value, (mine + k) % RING, 1, 0)
    up_ring = [(a, (a + stride) % z_len) for a in range(z_len)]
    down_ring = [(a, (a - stride) % z_len) for a in range(z_len)]
    far_up = along_z(chunk(up_now, 2), z_len, up_ring)
    far_down = along_z(chunk(down_now, 2), z_len, down_ring)
    next_up = along_z(jnp.concatenate([chunk(up_now, 1) + far_up, chunk(down_now, 1)], axis=1), z_len, up_ring)
    next_down = along_z(jnp.concatenate([chunk(up_now, 3), chunk(down_now, 3) + far_down], axis=1), z_len, down_ring)
    total = jnp.concatenate([chunk(up_now, 0), chunk(down_now, 0)], axis=1) + next_up + next_down
    a, b, c = X_UP, X_UP + Z_UP, 2 * X_UP + Z_UP
    return jnp.concatenate([total[:, :a], total[:, b:c], total[:, a:b], total[:, c:]], axis=1)


def reduce_input(gi, n_tensor):
    y_len = n_tensor // (X_HI * CORES)
    half = gi.shape[0] // 2
    both = lax.ppermute(gi[half:], "tensor", [(i, i ^ 1) for i in range(n_tensor)]) + gi[:half]
    groups = [
        [(x * y_len + y) * CORES + c for y in range(y_len)] for x in range(X_HI) for c in range(CORES)
    ]
    part = lax.psum_scatter(both, "tensor", scatter_dimension=0, axis_index_groups=groups, tiled=True)
    last = part.shape[0] // 2
    far = n_tensor // X_HI
    return lax.ppermute(part[last:], "tensor", [(i, (i + far) % n_tensor) for i in range(n_tensor)]) + part[:last]


def on_device(n_dp, n_tensor, activations, grad_hidden, weight_tiles, tile_slots, owner_map):
    tok_rows, width = activations.shape
    n_tiles = tile_slots.shape[1]
    n_cols = grad_hidden.shape[1] // TILE
    row_panels = width // TILE
    z_len = n_dp // X_LO
    y_len = n_tensor // (X_HI * CORES)
    dp, tp = lax.axis_index("dp"), lax.axis_index("tensor")
    other_x = (owner_map // z_len) ^ (dp // z_len)
    owner_z = owner_map % z_len
    other_z = (owner_z ^ dp) & 1
    stride, chunk = 2, jnp.zeros_like(owner_z)
    while z_len // stride > RING:
        chunk = chunk * 2 + (owner_z // stride) % 2
        stride *= 2
    chunk = chunk * RING + owner_z // stride
    n = z_len // 2
    places = jnp.concatenate([other_x * 2 * n + other_z * n + chunk, other_z * 2 * n + other_x * n + chunk], axis=0)
    per = row_panels // n_tensor
    row = tile_slots // n_cols
    owner = row // per
    core, y, x_hi = owner % CORES, (owner // CORES) % y_len, owner // (CORES * y_len)
    spots = (((core ^ (tp % CORES)) * y_len + y) * X_HI + (x_hi ^ (tp // (CORES * y_len)))) * per + row % per

    vmem = pl.BlockSpec(memory_space=pltpu.VMEM)
    smem = pl.BlockSpec(memory_space=pltpu.SMEM)
    params = pltpu.CompilerParams(vmem_limit_bytes=32 * 1024 * 1024)
    flops = 2 * n_tiles * tok_rows * TILE * TILE
    gp, xf, up, down = pl.pallas_call(
        functools.partial(weight_kernel, n_tiles, n_cols),
        out_shape=(
            jax.ShapeDtypeStruct((n_cols, tok_rows, TILE), jnp.bfloat16),
            jax.ShapeDtypeStruct((n_tiles, X_ROWS, TILE), jnp.float32),
            jax.ShapeDtypeStruct((n_tiles, Z_UP, TILE), jnp.float32),
            jax.ShapeDtypeStruct((n_tiles, Z_ROWS - Z_UP, TILE), jnp.float32),
        ),
        in_specs=[smem, smem, vmem, vmem, vmem],
        out_specs=(vmem, vmem, vmem, vmem),
        scratch_shapes=[pltpu.VMEM((n_cols, tok_rows, TILE), jnp.float32)],
        compiler_params=params,
        cost_estimate=pl.CostEstimate(flops=2 * flops, bytes_accessed=8 * 2**20, transcendentals=0),
    )(tile_slots, places, activations, grad_hidden, weight_tiles[0])
    gi = pl.pallas_call(
        functools.partial(input_kernel, n_tiles, n_cols),
        out_shape=jax.ShapeDtypeStruct((row_panels, tok_rows, TILE), jnp.float32),
        in_specs=[smem, smem, vmem, vmem],
        out_specs=vmem,
        compiler_params=params,
        cost_estimate=pl.CostEstimate(flops=flops, bytes_accessed=6 * 2**20, transcendentals=0),
    )(tile_slots, spots, gp, weight_tiles[0])
    grad_weight = reduce_weight(xf, up, down, z_len)
    panels = reduce_input(gi, n_tensor)
    grad_input = panels.transpose(1, 0, 2).reshape(tok_rows, per * TILE)
    return grad_input, grad_weight


def solution(mesh):
    return jax.shard_map(
        functools.partial(on_device, mesh.shape["dp"], mesh.shape["tensor"]),
        mesh=mesh,
        in_specs=(
            P("dp", None),
            P("dp", "tensor"),
            P("tensor", None, None, None),
            P("tensor", None),
            P("tensor", None),
        ),
        out_specs=(P("dp", "tensor"), P("dp", "tensor", None)),
        check_vma=False,
    )
```

```python
import functools

import jax
import jax.numpy as jnp
from jax import lax
from jax.experimental import pallas as pl
from jax.experimental.pallas import tpu as pltpu
from jax.sharding import PartitionSpec as P

TILE = 128
GROUP = 8
TILE_COPIES = 4
ROWS = (64, 64)
X_LO, X_HI, CORES = 2, 2, 2
RING = 8
VMEM_LIMIT = 58 * 2**20

root_two_pi = 0.7978845608028654
cubic_term = 0.044715


def gelu_slope(preact):
    inner = root_two_pi * (preact + cubic_term * preact * preact * preact)
    tangent = jnp.tanh(inner)
    return 0.5 * (1.0 + tangent) + 0.5 * preact * (1.0 - tangent * tangent) * root_two_pi * (
        1.0 + 3.0 * cubic_term * preact * preact
    )


def panel(index):
    return pl.ds(pl.multiple_of(index * TILE, TILE), TILE)


def tile_place(owner, here, z_len):
    other_x = (owner // z_len) ^ (here // z_len)
    owner_z = owner % z_len
    other_z = (owner_z ^ here) & 1
    stride, chunk = 2, 0
    while z_len // stride > RING:
        chunk = chunk * 2 + (owner_z // stride) % 2
        stride *= 2
    return (other_z * 2 + other_x) * (z_len // 2) + chunk * RING + owner_z // stride


def tile_copies(tiles_hbm, tiles_ref, sems):
    n = tiles_ref.shape[0] // TILE_COPIES
    return [
        pltpu.make_async_copy(tiles_hbm.at[pl.ds(k * n, n)], tiles_ref.at[pl.ds(k * n, n)], sems.at[k])
        for k in range(TILE_COPIES)
    ]


def tile_kernel(
    n_tiles, n_cols, per, z_len, y_len, slots_hbm, owners_hbm, x_hbm, g_hbm, tiles_hbm, send_hbm, keep_hbm, *refs
):
    outs, refs = refs[:2 * len(ROWS)], refs[2 * len(ROWS):]
    x_ref, g_ref, tiles_ref, pre_ref, gp_ref, gi_ref, slots, owners, order, sems = refs
    x_copy = pltpu.make_async_copy(x_hbm, x_ref, sems.at[TILE_COPIES])
    g_copy = pltpu.make_async_copy(g_hbm, g_ref, sems.at[TILE_COPIES + 1])
    scalars = [
        pltpu.make_async_copy(slots_hbm, slots, sems.at[TILE_COPIES + 2]),
        pltpu.make_async_copy(owners_hbm, owners, sems.at[TILE_COPIES + 3]),
    ]
    arriving = tile_copies(tiles_hbm, tiles_ref, sems)
    for copy in (*scalars, x_copy, *arriving, g_copy):
        copy.start()
    pre_ref[...] = jnp.zeros_like(pre_ref)
    gi_ref[...] = jnp.zeros_like(gi_ref)
    here = lax.axis_index("dp")
    for copy in scalars:
        copy.wait()

    def note(i, carry):
        order[tile_place(owners[0, i], here, z_len)] = i
        return carry

    lax.fori_loop(0, n_tiles, note, 0)
    x_copy.wait()

    def project(step, carry):
        products = []
        for k in range(GROUP):
            i = step * GROUP + k
            slot = slots[0, i]
            products.append((slot % n_cols, jnp.dot(
                x_ref[:, panel(slot // n_cols)], tiles_ref[i], preferred_element_type=jnp.float32
            )))
        for col, product in products:
            pre_ref[col] += product
        return carry

    steps = n_tiles // TILE_COPIES // GROUP
    for k in range(TILE_COPIES):
        arriving[k].wait()
        lax.fori_loop(k * steps, (k + 1) * steps, project, 0)
    g_copy.wait()
    for col in range(n_cols):
        grad = g_ref[:, col * TILE:(col + 1) * TILE].astype(jnp.float32)
        gp_ref[col] = (grad * gelu_slope(pre_ref[col])).astype(jnp.bfloat16)

    near = lax.axis_index("tensor")

    def back(step, carry):
        products = []
        for k in range(GROUP):
            i = step * GROUP + k
            row = slots[0, i] // n_cols
            owner = row // per
            core, y, x_hi = owner % CORES, (owner // CORES) % y_len, owner // (CORES * y_len)
            core, x_hi = core ^ (near % CORES), x_hi ^ (near // (CORES * y_len))
            products.append((((core * y_len + y) * X_HI + x_hi) * per + row % per, lax.dot_general(
                gp_ref[slots[0, i] % n_cols], tiles_ref[i],
                (((1,), (1,)), ((), ())), preferred_element_type=jnp.float32,
            )))
        for spot, product in products:
            gi_ref[spot] += product
        return carry

    lax.fori_loop(0, n_tiles // GROUP, back, 0)
    half = gi_ref.shape[0] // 2
    leaving = [
        pltpu.make_async_copy(gi_ref.at[pl.ds(half, half)], send_hbm, sems.at[TILE_COPIES + 4]),
        pltpu.make_async_copy(gi_ref.at[pl.ds(0, half)], keep_hbm, sems.at[TILE_COPIES + 5]),
    ]
    for copy in leaving:
        copy.start()

    n = z_len // 2
    for kind in range(4):
        other_z, other_x = kind // 2, kind % 2

        def weight_grad(step, carry):
            for k in range(GROUP):
                place = kind * n + step * GROUP + k
                slot = slots[0, order[place]]
                product = lax.dot_general(
                    x_ref[:, panel(slot // n_cols)], gp_ref[slot % n_cols],
                    (((0,), (0,)), ((), ())), preferred_element_type=jnp.float32,
                )
                start = 0
                for p, rows in enumerate(ROWS):
                    outs[2 * p + other_z][other_x * n + step * GROUP + k] = product[start:start + rows]
                    start += rows
            return carry

        lax.fori_loop(0, n // GROUP, weight_grad, 0)
    for copy in leaving:
        copy.wait()


def along_z(value, sizes, move):
    n_dp, n_tensor = sizes
    z_len = n_dp // X_LO
    pairs = []
    for dp in range(n_dp):
        for tp in range(n_tensor):
            z = move(dp % z_len, tp % CORES) % z_len
            pairs.append((dp * n_tensor + tp, (dp - dp % z_len + z) * n_tensor + tp))
    return lax.ppermute(value, ("dp", "tensor"), pairs)


def partner(stride):
    return lambda z, core: z + stride * (1 - 2 * ((z // stride + core) % 2))


def swap_x(value, sizes):
    n_dp = sizes[0]
    return lax.ppermute(value, "dp", [(i, (i + n_dp // X_LO) % n_dp) for i in range(n_dp)])


def pick(value, at, count):
    return lax.dynamic_slice_in_dim(value, at * count, count, 0)


def swap_cores(value, sizes):
    return lax.ppermute(value, "tensor", [(i, i ^ 1) for i in range(sizes[1])])


def swap_x_hi(value, sizes):
    n_tensor = sizes[1]
    return lax.ppermute(value, "tensor", [(i, (i + n_tensor // X_HI) % n_tensor) for i in range(n_tensor)])


def sum_over_y(value, sizes):
    y_len = sizes[1] // (X_HI * CORES)
    groups = [
        [(x * y_len + y) * CORES + c for y in range(y_len)] for x in range(X_HI) for c in range(CORES)
    ]
    return lax.psum_scatter(value, "tensor", scatter_dimension=0, axis_index_groups=groups, tiled=True)


def reduce_all(parts, send, keep, sizes):
    z = lax.rem(lax.axis_index("dp"), sizes[0] // X_LO)
    core = lax.rem(lax.axis_index("tensor"), CORES)
    got_parts = [along_z(away, sizes, partner(1)) for away, _ in parts]
    panels = sum_over_y(swap_cores(send, sizes) + keep, sizes)
    sums = []
    for got, (_, here) in zip(got_parts, parts):
        n = got.shape[0] // 2
        now = got[:n] + here[:n] + swap_x(got[n:] + here[n:], sizes)
        stride = 2
        while now.shape[0] > RING:
            half, digit = now.shape[0] // 2, lax.rem(lax.div(z, stride), 2)
            now = pick(now, digit, half) + along_z(pick(now, 1 - digit, half), sizes, partner(stride))
            stride *= 2
        sums.append(now)
    now = jnp.concatenate(sums, axis=1)
    mine, way = lax.div(z, stride), 1 - 2 * core
    chunk = lambda k: pick(now, lax.rem(mine + k * way + RING, RING), 1)
    far, near, total = chunk(RING // 2), None, chunk(0)
    for k in range(RING // 2, 0, -1):
        if near is not None:
            far, near = lax.optimization_barrier((far, near))
        far = along_z(far, sizes, lambda z, core: z + stride * (1 - 2 * core))
        if near is not None:
            near = along_z(near, sizes, lambda z, core: z - stride * (1 - 2 * core))
        if k > 1:
            far = far + chunk(k - 1)
            near = chunk(1 - k) if near is None else near + chunk(1 - k)
    half = panels.shape[0] // 2
    panels = swap_x_hi(panels[half:], sizes) + panels[:half]
    return jnp.concatenate([panels[j] for j in range(half)], axis=1), total + far + near


def on_device(n_dp, n_tensor, activations, grad_hidden, weight_tiles, tile_slots, owner_map):
    tok_rows, width = activations.shape
    n_tiles = tile_slots.shape[1]
    n_cols = grad_hidden.shape[1] // TILE
    row_panels = width // TILE
    per = row_panels // n_tensor
    z_len = n_dp // X_LO
    y_len = n_tensor // (X_HI * CORES)
    hbm = pl.BlockSpec(memory_space=pl.ANY)
    vmem = pl.BlockSpec(memory_space=pltpu.VMEM)
    flops = 2 * n_tiles * tok_rows * TILE * TILE
    f32 = lambda *shape: jax.ShapeDtypeStruct(shape, jnp.float32)
    f32_parts = [f32(n_tiles // 2, rows, TILE) for rows in ROWS for _ in range(2)]
    send, keep, *parts = pl.pallas_call(
        functools.partial(tile_kernel, n_tiles, n_cols, per, z_len, y_len),
        out_shape=(f32(row_panels // 2, tok_rows, TILE), f32(row_panels // 2, tok_rows, TILE), *f32_parts),
        in_specs=[hbm] * 5,
        out_specs=(hbm, hbm) + (vmem,) * len(f32_parts),
        scratch_shapes=[
            pltpu.VMEM(activations.shape, jnp.bfloat16),
            pltpu.VMEM(grad_hidden.shape, jnp.bfloat16),
            pltpu.VMEM((n_tiles, TILE, TILE), jnp.bfloat16),
            pltpu.VMEM((n_cols, tok_rows, TILE), jnp.float32),
            pltpu.VMEM((n_cols, tok_rows, TILE), jnp.bfloat16),
            pltpu.VMEM((row_panels, tok_rows, TILE), jnp.float32),
            pltpu.SMEM((1, n_tiles), jnp.int32),
            pltpu.SMEM((1, n_tiles), jnp.int32),
            pltpu.SMEM((n_tiles,), jnp.int32),
            pltpu.SemaphoreType.DMA((6 + TILE_COPIES,)),
        ],
        compiler_params=pltpu.CompilerParams(vmem_limit_bytes=VMEM_LIMIT),
        cost_estimate=pl.CostEstimate(flops=3 * flops, bytes_accessed=12 * 2**20, transcendentals=0),
    )(tile_slots, owner_map, activations, grad_hidden, weight_tiles[0])
    pairs = [(parts[2 * p + 1], parts[2 * p]) for p in range(len(ROWS))]
    return reduce_all(pairs, send, keep, (n_dp, n_tensor))


def solution(mesh):
    return jax.shard_map(
        functools.partial(on_device, mesh.shape["dp"], mesh.shape["tensor"]),
        mesh=mesh,
        in_specs=(
            P("dp", None),
            P("dp", "tensor"),
            P("tensor", None, None, None),
            P("tensor", None),
            P("tensor", None),
        ),
        out_specs=(P("dp", "tensor"), P("dp", "tensor", None)),
        check_vma=False,
    )
```

```python
import functools

import jax
import jax.numpy as jnp
from jax import lax
from jax.experimental import pallas as pl
from jax.experimental.pallas import tpu as pltpu
from jax.sharding import PartitionSpec as P

TILE = 128
GROUP = 16
TILE_COPIES = 4
ROWS = (64, 64)
X_LO, X_HI, CORES = 2, 2, 2
RING = 4
VMEM_LIMIT = 58 * 2**20

root_two_pi = 0.7978845608028654
cubic_term = 0.044715


def gelu_slope(preact):
    inner = root_two_pi * (preact + cubic_term * preact * preact * preact)
    tangent = jnp.tanh(inner)
    return 0.5 * (1.0 + tangent) + 0.5 * preact * (1.0 - tangent * tangent) * root_two_pi * (
        1.0 + 3.0 * cubic_term * preact * preact
    )


def panel(index):
    return pl.ds(pl.multiple_of(index * TILE, TILE), TILE)


def split(value, by):
    quotient = (value * (-(-2**16 // by))) >> 16
    return quotient, value - quotient * by


def tile_place(owner, here, z_len):
    owner_x, owner_z = split(owner, z_len)
    other_x, other_z = owner_x ^ split(here, z_len)[0], (owner_z ^ here) & 1
    rest, _ = split(owner_z, 2)
    stride, chunk = 2, 0
    while z_len // stride > RING:
        rest, digit = split(rest, 2)
        chunk = chunk * 2 + digit
        stride *= 2
    return (other_z * 2 + other_x) * (z_len // 2) + chunk * RING + rest


def tile_copies(tiles_hbm, tiles_ref, sems):
    n = tiles_ref.shape[0] // TILE_COPIES
    return [
        pltpu.make_async_copy(tiles_hbm.at[pl.ds(k * n, n)], tiles_ref.at[pl.ds(k * n, n)], sems.at[k])
        for k in range(TILE_COPIES)
    ]


def tile_kernel(
    n_tiles, n_cols, per, z_len, y_len, slots_hbm, owners_hbm, x_hbm, g_hbm, tiles_hbm, send_hbm, keep_hbm, *refs
):
    outs, refs = refs[:2 * len(ROWS)], refs[2 * len(ROWS):]
    x_ref, g_ref, tiles_ref, pre_ref, gp_ref, gi_ref, slots, owners, order, row_of, col_of, sems = refs
    x_copy = pltpu.make_async_copy(x_hbm, x_ref, sems.at[TILE_COPIES])
    g_copy = pltpu.make_async_copy(g_hbm, g_ref, sems.at[TILE_COPIES + 1])
    scalars = [
        pltpu.make_async_copy(slots_hbm, slots, sems.at[TILE_COPIES + 2]),
        pltpu.make_async_copy(owners_hbm, owners, sems.at[TILE_COPIES + 3]),
    ]
    arriving = tile_copies(tiles_hbm, tiles_ref, sems)
    for copy in (*scalars, x_copy, *arriving, g_copy):
        copy.start()
    pre_ref[...] = jnp.zeros_like(pre_ref)
    gi_ref[...] = jnp.zeros_like(gi_ref)
    here = lax.axis_index("dp")
    for copy in scalars:
        copy.wait()

    x_copy.wait()

    def project(step, carry):
        products = []
        for k in range(GROUP):
            i = step * GROUP + k
            row, col = split(slots[0, i], n_cols)
            order[tile_place(owners[0, i], here, z_len)] = i
            row_of[i], col_of[i] = row, col
            products.append((col, jnp.dot(
                x_ref[:, panel(row)], tiles_ref[i], preferred_element_type=jnp.float32
            )))
        for col, product in products:
            pre_ref[col] += product
        return carry

    steps = n_tiles // TILE_COPIES // GROUP
    for k in range(TILE_COPIES):
        arriving[k].wait()
        lax.fori_loop(k * steps, (k + 1) * steps, project, 0)
    g_copy.wait()
    for col in range(n_cols):
        grad = g_ref[:, col * TILE:(col + 1) * TILE].astype(jnp.float32)
        gp_ref[col] = (grad * gelu_slope(pre_ref[col])).astype(jnp.bfloat16)

    near = lax.axis_index("tensor")

    def back(step, carry):
        products = []
        for k in range(GROUP):
            i = step * GROUP + k
            owner, spot = split(row_of[i], per)
            owner, core = split(owner, CORES)
            x_hi, y = split(owner, y_len)
            spot = (((core ^ (near & 1)) * y_len + y) * X_HI + x_hi) * per + spot
            products.append((spot, lax.dot_general(
                gp_ref[col_of[i]], tiles_ref[i],
                (((1,), (1,)), ((), ())), preferred_element_type=jnp.float32,
            )))
        for spot, product in products:
            gi_ref[spot] += product
        return carry

    lax.fori_loop(0, n_tiles // GROUP, back, 0)
    half = gi_ref.shape[0] // 2
    leaving = [
        pltpu.make_async_copy(gi_ref.at[pl.ds(half, half)], send_hbm, sems.at[TILE_COPIES + 4]),
        pltpu.make_async_copy(gi_ref.at[pl.ds(0, half)], keep_hbm, sems.at[TILE_COPIES + 5]),
    ]
    for copy in leaving:
        copy.start()

    n = z_len // 2
    for kind in range(4):
        other_z, other_x = kind // 2, kind % 2

        def weight_grad(step, carry):
            for k in range(GROUP):
                place = kind * n + step * GROUP + k
                i = order[place]
                product = lax.dot_general(
                    x_ref[:, panel(row_of[i])], gp_ref[col_of[i]],
                    (((0,), (0,)), ((), ())), preferred_element_type=jnp.float32,
                )
                start = 0
                for p, rows in enumerate(ROWS):
                    outs[2 * p + other_z][other_x * n + step * GROUP + k] = product[start:start + rows]
                    start += rows
            return carry

        lax.fori_loop(0, n // GROUP, weight_grad, 0)
    for copy in leaving:
        copy.wait()


def along_z(value, sizes, move):
    n_dp, n_tensor = sizes
    z_len = n_dp // X_LO
    pairs = []
    for dp in range(n_dp):
        for tp in range(n_tensor):
            z = move(dp % z_len, tp % CORES) % z_len
            pairs.append((dp * n_tensor + tp, (dp - dp % z_len + z) * n_tensor + tp))
    return lax.ppermute(value, ("dp", "tensor"), pairs)


def partner(stride):
    return lambda z, core: z + stride * (1 - 2 * ((z // stride + core) % 2))


def swap_x(value, sizes):
    n_dp = sizes[0]
    return lax.ppermute(value, "dp", [(i, (i + n_dp // X_LO) % n_dp) for i in range(n_dp)])


def pick(value, at, count):
    return lax.dynamic_slice_in_dim(value, at * count, count, 0)


def swap_cores(value, sizes):
    return lax.ppermute(value, "tensor", [(i, i ^ 1) for i in range(sizes[1])])


def sum_over(value, axis, sizes):
    y_len = sizes[1] // (X_HI * CORES)
    index = lambda x, y, c: (x * y_len + y) * CORES + c
    if axis == "y":
        groups = [[index(x, y, c) for y in range(y_len)] for x in range(X_HI) for c in range(CORES)]
    else:
        groups = [[index(x, y, c) for x in range(X_HI)] for y in range(y_len) for c in range(CORES)]
    return lax.psum_scatter(value, "tensor", scatter_dimension=0, axis_index_groups=groups, tiled=True)


def reduce_all(parts, send, keep, sizes):
    z = lax.rem(lax.axis_index("dp"), sizes[0] // X_LO)
    core = lax.rem(lax.axis_index("tensor"), CORES)
    got_parts = [along_z(away, sizes, partner(1)) for away, _ in parts]
    panels = sum_over(swap_cores(send, sizes) + keep, "y", sizes)
    sums = []
    for got, (_, here) in zip(got_parts, parts):
        n = got.shape[0] // 2
        sums.append(got[:n] + here[:n] + swap_x(got[n:] + here[n:], sizes))
    stride = 2
    while sums[0].shape[0] > RING:
        half, digit = sums[0].shape[0] // 2, lax.rem(lax.div(z, stride), 2)
        if half == RING:
            sums[-1], panels = lax.optimization_barrier((sums[-1], panels))
            panels = sum_over(panels, "x_hi", sizes)
        sums = [
            pick(now, digit, half) + along_z(pick(now, 1 - digit, half), sizes, partner(stride)) for now in sums
        ]
        stride *= 2
    now = jnp.concatenate(sums, axis=1)
    panels = jnp.concatenate([panels[j] for j in range(panels.shape[0])], axis=1)
    mine, way = lax.div(z, stride), 1 - 2 * core
    chunk = lambda k: pick(now, lax.rem(mine + k * way + RING, RING), 1)
    far, near, total = chunk(RING // 2), None, chunk(0)
    for k in range(RING // 2, 0, -1):
        if near is not None:
            far, near = lax.optimization_barrier((far, near))
            near = along_z(near, sizes, lambda z, core: z - stride * (1 - 2 * core))
        far = along_z(far, sizes, lambda z, core: z + stride * (1 - 2 * core))
        if k > 1:
            far = far + chunk(k - 1)
            near = chunk(1 - k) if near is None else near + chunk(1 - k)
    far, near, panels = lax.optimization_barrier((far, near, panels))
    return panels, total + far + near


def on_device(n_dp, n_tensor, activations, grad_hidden, weight_tiles, tile_slots, owner_map):
    tok_rows, width = activations.shape
    n_tiles = tile_slots.shape[1]
    n_cols = grad_hidden.shape[1] // TILE
    row_panels = width // TILE
    per = row_panels // n_tensor
    z_len = n_dp // X_LO
    y_len = n_tensor // (X_HI * CORES)
    hbm = pl.BlockSpec(memory_space=pl.ANY)
    vmem = pl.BlockSpec(memory_space=pltpu.VMEM)
    flops = 2 * n_tiles * tok_rows * TILE * TILE
    f32 = lambda *shape: jax.ShapeDtypeStruct(shape, jnp.float32)
    f32_parts = [f32(n_tiles // 2, rows, TILE) for rows in ROWS for _ in range(2)]
    send, keep, *parts = pl.pallas_call(
        functools.partial(tile_kernel, n_tiles, n_cols, per, z_len, y_len),
        out_shape=(f32(row_panels // 2, tok_rows, TILE), f32(row_panels // 2, tok_rows, TILE), *f32_parts),
        in_specs=[hbm] * 5,
        out_specs=(hbm, hbm) + (vmem,) * len(f32_parts),
        scratch_shapes=[
            pltpu.VMEM(activations.shape, jnp.bfloat16),
            pltpu.VMEM(grad_hidden.shape, jnp.bfloat16),
            pltpu.VMEM((n_tiles, TILE, TILE), jnp.bfloat16),
            pltpu.VMEM((n_cols, tok_rows, TILE), jnp.float32),
            pltpu.VMEM((n_cols, tok_rows, TILE), jnp.bfloat16),
            pltpu.VMEM((row_panels, tok_rows, TILE), jnp.float32),
            pltpu.SMEM((1, n_tiles), jnp.int32),
            pltpu.SMEM((1, n_tiles), jnp.int32),
            *[pltpu.SMEM((n_tiles,), jnp.int32)] * 3,
            pltpu.SemaphoreType.DMA((6 + TILE_COPIES,)),
        ],
        compiler_params=pltpu.CompilerParams(vmem_limit_bytes=VMEM_LIMIT),
        cost_estimate=pl.CostEstimate(flops=3 * flops, bytes_accessed=12 * 2**20, transcendentals=0),
    )(tile_slots, owner_map, activations, grad_hidden, weight_tiles[0])
    pairs = [(parts[2 * p + 1], parts[2 * p]) for p in range(len(ROWS))]
    return reduce_all(pairs, send, keep, (n_dp, n_tensor))


def solution(mesh):
    return jax.shard_map(
        functools.partial(on_device, mesh.shape["dp"], mesh.shape["tensor"]),
        mesh=mesh,
        in_specs=(
            P("dp", None),
            P("dp", "tensor"),
            P("tensor", None, None, None),
            P("tensor", None),
            P("tensor", None),
        ),
        out_specs=(P("dp", "tensor"), P("dp", "tensor", None)),
        check_vma=False,
    )
```

```python
import functools

import jax
import jax.numpy as jnp
from jax import lax
from jax.experimental import pallas as pl
from jax.experimental.pallas import tpu as pltpu
from jax.sharding import PartitionSpec as P

TILE = 128
GROUP = 16
TILE_COPIES = 4
ROWS = (48, 32, 48)
X_FIRST = (False, True, False)
GROUPED = ((0, 1), (2,))
X_LO, X_HI, CORES = 2, 2, 2
RING = 4
VMEM_LIMIT = 58 * 2**20

root_two_pi = 0.7978845608028654
cubic_term = 0.044715


def gelu_slope(preact):
    inner = root_two_pi * (preact + cubic_term * preact * preact * preact)
    tangent = jnp.tanh(inner)
    return 0.5 * (1.0 + tangent) + 0.5 * preact * (1.0 - tangent * tangent) * root_two_pi * (
        1.0 + 3.0 * cubic_term * preact * preact
    )


def panel(index):
    return pl.ds(pl.multiple_of(index * TILE, TILE), TILE)


def split(value, by):
    quotient = (value * (-(-2**16 // by))) >> 16
    return quotient, value - quotient * by


def tile_place(owner, here, z_len):
    owner_x, owner_z = split(owner, z_len)
    other_x, other_z = owner_x ^ split(here, z_len)[0], (owner_z ^ here) & 1
    rest, _ = split(owner_z, 2)
    stride, chunk = 2, 0
    while z_len // stride > RING:
        rest, digit = split(rest, 2)
        chunk = chunk * 2 + digit
        stride *= 2
    return (other_z * 2 + other_x) * (z_len // 2) + chunk * RING + rest


def tile_copies(tiles_hbm, tiles_ref, sems):
    n = tiles_ref.shape[0] // TILE_COPIES
    return [
        pltpu.make_async_copy(tiles_hbm.at[pl.ds(k * n, n)], tiles_ref.at[pl.ds(k * n, n)], sems.at[k])
        for k in range(TILE_COPIES)
    ]


def tile_kernel(
    n_tiles, n_cols, per, z_len, y_len, slots_hbm, owners_hbm, x_hbm, g_hbm, tiles_hbm, send_hbm, keep_hbm, *refs
):
    outs, refs = refs[:2 * len(ROWS)], refs[2 * len(ROWS):]
    x_ref, g_ref, tiles_ref, pre_ref, gp_ref, gi_ref, slots, owners, order, row_of, col_of, sems = refs
    x_copy = pltpu.make_async_copy(x_hbm, x_ref, sems.at[TILE_COPIES])
    g_copy = pltpu.make_async_copy(g_hbm, g_ref, sems.at[TILE_COPIES + 1])
    scalars = [
        pltpu.make_async_copy(slots_hbm, slots, sems.at[TILE_COPIES + 2]),
        pltpu.make_async_copy(owners_hbm, owners, sems.at[TILE_COPIES + 3]),
    ]
    arriving = tile_copies(tiles_hbm, tiles_ref, sems)
    for copy in (*scalars, x_copy, *arriving, g_copy):
        copy.start()
    pre_ref[...] = jnp.zeros_like(pre_ref)
    gi_ref[...] = jnp.zeros_like(gi_ref)
    here = lax.axis_index("dp")
    for copy in scalars:
        copy.wait()

    x_copy.wait()

    def project(step, carry):
        products = []
        for k in range(GROUP):
            i = step * GROUP + k
            row, col = split(slots[0, i], n_cols)
            order[tile_place(owners[0, i], here, z_len)] = i
            row_of[i], col_of[i] = row, col
            products.append((col, jnp.dot(
                x_ref[:, panel(row)], tiles_ref[i], preferred_element_type=jnp.float32
            )))
        for col, product in products:
            pre_ref[col] += product
        return carry

    steps = n_tiles // TILE_COPIES // GROUP
    for k in range(TILE_COPIES):
        arriving[k].wait()
        lax.fori_loop(k * steps, (k + 1) * steps, project, 0)
    g_copy.wait()
    for col in range(n_cols):
        grad = g_ref[:, col * TILE:(col + 1) * TILE].astype(jnp.float32)
        gp_ref[col] = (grad * gelu_slope(pre_ref[col])).astype(jnp.bfloat16)

    near = lax.axis_index("tensor")

    def back(step, carry):
        products = []
        for k in range(GROUP):
            i = step * GROUP + k
            owner, spot = split(row_of[i], per)
            owner, core = split(owner, CORES)
            x_hi, y = split(owner, y_len)
            spot = (((core ^ (near & 1)) * y_len + y) * X_HI + x_hi) * per + spot
            products.append((spot, lax.dot_general(
                gp_ref[col_of[i]], tiles_ref[i],
                (((1,), (1,)), ((), ())), preferred_element_type=jnp.float32,
            )))
        for spot, product in products:
            gi_ref[spot] += product
        return carry

    lax.fori_loop(0, n_tiles // GROUP, back, 0)
    half = gi_ref.shape[0] // 2
    leaving = [
        pltpu.make_async_copy(gi_ref.at[pl.ds(half, half)], send_hbm, sems.at[TILE_COPIES + 4]),
        pltpu.make_async_copy(gi_ref.at[pl.ds(0, half)], keep_hbm, sems.at[TILE_COPIES + 5]),
    ]
    for copy in leaving:
        copy.start()

    n = z_len // 2
    for kind in range(4):
        other_z, other_x = kind // 2, kind % 2

        def weight_grad(step, carry):
            for k in range(GROUP):
                place = kind * n + step * GROUP + k
                i = order[place]
                product = lax.dot_general(
                    x_ref[:, panel(row_of[i])], gp_ref[col_of[i]],
                    (((0,), (0,)), ((), ())), preferred_element_type=jnp.float32,
                )
                start = 0
                for p, rows in enumerate(ROWS):
                    first, second = (other_x, other_z) if X_FIRST[p] else (other_z, other_x)
                    outs[2 * p + first][second * n + step * GROUP + k] = product[start:start + rows]
                    start += rows
            return carry

        lax.fori_loop(0, n // GROUP, weight_grad, 0)
    for copy in leaving:
        copy.wait()


def along_z(value, sizes, move):
    n_dp, n_tensor = sizes
    z_len = n_dp // X_LO
    pairs = []
    for dp in range(n_dp):
        for tp in range(n_tensor):
            z = move(dp % z_len, tp % CORES) % z_len
            pairs.append((dp * n_tensor + tp, (dp - dp % z_len + z) * n_tensor + tp))
    return lax.ppermute(value, ("dp", "tensor"), pairs)


def partner(stride):
    return lambda z, core: z + stride * (1 - 2 * ((z // stride + core) % 2))


def swap_x(value, sizes):
    n_dp = sizes[0]
    return lax.ppermute(value, "dp", [(i, (i + n_dp // X_LO) % n_dp) for i in range(n_dp)])


def pick(value, at, count):
    return lax.dynamic_slice_in_dim(value, at * count, count, 0)


def swap_cores(value, sizes):
    return lax.ppermute(value, "tensor", [(i, i ^ 1) for i in range(sizes[1])])


def sum_over(value, axis, sizes):
    y_len = sizes[1] // (X_HI * CORES)
    index = lambda x, y, c: (x * y_len + y) * CORES + c
    if axis == "y":
        groups = [[index(x, y, c) for y in range(y_len)] for x in range(X_HI) for c in range(CORES)]
    else:
        groups = [[index(x, y, c) for x in range(X_HI)] for y in range(y_len) for c in range(CORES)]
    return lax.psum_scatter(value, "tensor", scatter_dimension=0, axis_index_groups=groups, tiled=True)


def reduce_all(parts, send, keep, sizes):
    z = lax.rem(lax.axis_index("dp"), sizes[0] // X_LO)
    core = lax.rem(lax.axis_index("tensor"), CORES)
    pair_z = lambda value: along_z(value, sizes, partner(1))
    pair_x = lambda value: swap_x(value, sizes)
    got_parts = [(pair_x if x_first else pair_z)(away) for (away, _), x_first in zip(parts, X_FIRST)]
    panels = sum_over(swap_cores(send, sizes) + keep, "y", sizes)
    sums = []
    for got, (_, here), x_first in zip(got_parts, parts, X_FIRST):
        n = got.shape[0] // 2
        sums.append(got[:n] + here[:n] + (pair_z if x_first else pair_x)(got[n:] + here[n:]))
    sums = [jnp.concatenate([sums[p] for p in group], axis=1) for group in GROUPED]
    stride = 2
    while sums[0].shape[0] > RING:
        half, digit = sums[0].shape[0] // 2, lax.rem(lax.div(z, stride), 2)
        if half == RING:
            sums[-1], panels = lax.optimization_barrier((sums[-1], panels))
            panels = sum_over(panels, "x_hi", sizes)
        sums = [
            pick(now, digit, half) + along_z(pick(now, 1 - digit, half), sizes, partner(stride)) for now in sums
        ]
        stride *= 2
    now = jnp.concatenate(sums, axis=1)
    panels = jnp.concatenate([panels[j] for j in range(panels.shape[0])], axis=1)
    mine, way = lax.div(z, stride), 1 - 2 * core
    chunk = lambda k: pick(now, lax.rem(mine + k * way + RING, RING), 1)
    far, near, total = chunk(RING // 2), None, chunk(0)
    for k in range(RING // 2, 0, -1):
        if near is not None:
            far, near = lax.optimization_barrier((far, near))
            near = along_z(near, sizes, lambda z, core: z - stride * (1 - 2 * core))
        far = along_z(far, sizes, lambda z, core: z + stride * (1 - 2 * core))
        if k > 1:
            far = far + chunk(k - 1)
            near = chunk(1 - k) if near is None else near + chunk(1 - k)
    far, near, panels = lax.optimization_barrier((far, near, panels))
    return panels, total + far + near


def on_device(n_dp, n_tensor, activations, grad_hidden, weight_tiles, tile_slots, owner_map):
    tok_rows, width = activations.shape
    n_tiles = tile_slots.shape[1]
    n_cols = grad_hidden.shape[1] // TILE
    row_panels = width // TILE
    per = row_panels // n_tensor
    z_len = n_dp // X_LO
    y_len = n_tensor // (X_HI * CORES)
    hbm = pl.BlockSpec(memory_space=pl.ANY)
    vmem = pl.BlockSpec(memory_space=pltpu.VMEM)
    flops = 2 * n_tiles * tok_rows * TILE * TILE
    f32 = lambda *shape: jax.ShapeDtypeStruct(shape, jnp.float32)
    f32_parts = [f32(n_tiles // 2, rows, TILE) for rows in ROWS for _ in range(2)]
    send, keep, *parts = pl.pallas_call(
        functools.partial(tile_kernel, n_tiles, n_cols, per, z_len, y_len),
        out_shape=(f32(row_panels // 2, tok_rows, TILE), f32(row_panels // 2, tok_rows, TILE), *f32_parts),
        in_specs=[hbm] * 5,
        out_specs=(hbm, hbm) + (vmem,) * len(f32_parts),
        scratch_shapes=[
            pltpu.VMEM(activations.shape, jnp.bfloat16),
            pltpu.VMEM(grad_hidden.shape, jnp.bfloat16),
            pltpu.VMEM((n_tiles, TILE, TILE), jnp.bfloat16),
            pltpu.VMEM((n_cols, tok_rows, TILE), jnp.float32),
            pltpu.VMEM((n_cols, tok_rows, TILE), jnp.bfloat16),
            pltpu.VMEM((row_panels, tok_rows, TILE), jnp.float32),
            pltpu.SMEM((1, n_tiles), jnp.int32),
            pltpu.SMEM((1, n_tiles), jnp.int32),
            *[pltpu.SMEM((n_tiles,), jnp.int32)] * 3,
            pltpu.SemaphoreType.DMA((6 + TILE_COPIES,)),
        ],
        compiler_params=pltpu.CompilerParams(vmem_limit_bytes=VMEM_LIMIT),
        cost_estimate=pl.CostEstimate(flops=3 * flops, bytes_accessed=12 * 2**20, transcendentals=0),
    )(tile_slots, owner_map, activations, grad_hidden, weight_tiles[0])
    pairs = [(parts[2 * p + 1], parts[2 * p]) for p in range(len(ROWS))]
    return reduce_all(pairs, send, keep, (n_dp, n_tensor))


def solution(mesh):
    return jax.shard_map(
        functools.partial(on_device, mesh.shape["dp"], mesh.shape["tensor"]),
        mesh=mesh,
        in_specs=(
            P("dp", None),
            P("dp", "tensor"),
            P("tensor", None, None, None),
            P("tensor", None),
            P("tensor", None),
        ),
        out_specs=(P("dp", "tensor"), P("dp", "tensor", None)),
        check_vma=False,
    )
```

```python
import functools

import jax
import jax.numpy as jnp
from jax import lax
from jax.experimental import pallas as pl
from jax.experimental.pallas import tpu as pltpu
from jax.sharding import PartitionSpec as P

TILE = 128
GROUP = 16
TILE_COPIES = 4
ROWS = (48, 32, 48)
X_FIRST = (False, True, False)
GROUPED = ((0, 1), (2,))
X_LO, X_HI, CORES = 2, 2, 2
RING = 4
VMEM_LIMIT = 58 * 2**20

root_two_pi = 0.7978845608028654
cubic_term = 0.044715


def gelu_slope(preact):
    inner = root_two_pi * (preact + cubic_term * preact * preact * preact)
    tangent = jnp.tanh(inner)
    return 0.5 * (1.0 + tangent) + 0.5 * preact * (1.0 - tangent * tangent) * root_two_pi * (
        1.0 + 3.0 * cubic_term * preact * preact
    )


def panel(index):
    return pl.ds(pl.multiple_of(index * TILE, TILE), TILE)


def split(value, by):
    quotient = (value * (-(-2**16 // by))) >> 16
    return quotient, value - quotient * by


def tile_place(owner, here, z_len):
    owner_x, owner_z = split(owner, z_len)
    other_x, other_z = owner_x ^ split(here, z_len)[0], (owner_z ^ here) & 1
    rest, _ = split(owner_z, 2)
    stride, chunk = 2, 0
    while z_len // stride > RING:
        rest, digit = split(rest, 2)
        chunk = chunk * 2 + digit
        stride *= 2
    return (other_z * 2 + other_x) * (z_len // 2) + chunk * RING + rest


def tile_copies(tiles_hbm, tiles_ref, sems):
    n = tiles_ref.shape[0] // TILE_COPIES
    return [
        pltpu.make_async_copy(tiles_hbm.at[pl.ds(k * n, n)], tiles_ref.at[pl.ds(k * n, n)], sems.at[k])
        for k in range(TILE_COPIES)
    ]


def tile_kernel(
    n_tiles, n_cols, per, z_len, y_len, slots_hbm, owners_hbm, x_hbm, g_hbm, tiles_hbm, send_hbm, keep_hbm, *refs
):
    outs, refs = refs[:2 * len(ROWS)], refs[2 * len(ROWS):]
    x_ref, g_ref, tiles_ref, pre_ref, gp_ref, gi_ref, slots, owners, order, row_of, col_of, sems = refs
    x_copy = pltpu.make_async_copy(x_hbm, x_ref, sems.at[TILE_COPIES])
    g_copy = pltpu.make_async_copy(g_hbm, g_ref, sems.at[TILE_COPIES + 1])
    scalars = [
        pltpu.make_async_copy(slots_hbm, slots, sems.at[TILE_COPIES + 2]),
        pltpu.make_async_copy(owners_hbm, owners, sems.at[TILE_COPIES + 3]),
    ]
    arriving = tile_copies(tiles_hbm, tiles_ref, sems)
    for copy in (*scalars, x_copy, *arriving, g_copy):
        copy.start()
    pre_ref[...] = jnp.zeros_like(pre_ref)
    gi_ref[...] = jnp.zeros_like(gi_ref)
    here = lax.axis_index("dp")
    for copy in scalars:
        copy.wait()

    x_copy.wait()

    def project(step, carry):
        products = []
        for k in range(GROUP):
            i = step * GROUP + k
            row, col = split(slots[0, i], n_cols)
            order[tile_place(owners[0, i], here, z_len)] = i
            row_of[i], col_of[i] = row, col
            products.append((col, jnp.dot(
                x_ref[:, panel(row)], tiles_ref[i], preferred_element_type=jnp.float32
            )))
        for col, product in products:
            pre_ref[col] += product
        return carry

    steps = n_tiles // TILE_COPIES // GROUP
    for k in range(TILE_COPIES):
        arriving[k].wait()
        lax.fori_loop(k * steps, (k + 1) * steps, project, 0)
    g_copy.wait()
    for col in range(n_cols):
        grad = g_ref[:, col * TILE:(col + 1) * TILE].astype(jnp.float32)
        gp_ref[col] = (grad * gelu_slope(pre_ref[col])).astype(jnp.bfloat16)

    near = lax.axis_index("tensor")

    def back(step, carry):
        products = []
        for k in range(GROUP):
            i = step * GROUP + k
            owner, spot = split(row_of[i], per)
            owner, core = split(owner, CORES)
            x_hi, y = split(owner, y_len)
            spot = (((core ^ (near & 1)) * y_len + y) * X_HI + x_hi) * per + spot
            products.append((spot, lax.dot_general(
                gp_ref[col_of[i]], tiles_ref[i],
                (((1,), (1,)), ((), ())), preferred_element_type=jnp.float32,
            )))
        for spot, product in products:
            gi_ref[spot] += product
        return carry

    lax.fori_loop(0, n_tiles // GROUP, back, 0)
    half = gi_ref.shape[0] // 2
    leaving = [
        pltpu.make_async_copy(gi_ref.at[pl.ds(half, half)], send_hbm, sems.at[TILE_COPIES + 4]),
        pltpu.make_async_copy(gi_ref.at[pl.ds(0, half)], keep_hbm, sems.at[TILE_COPIES + 5]),
    ]
    for copy in leaving:
        copy.start()

    n = z_len // 2
    for kind in range(4):
        other_z, other_x = kind // 2, kind % 2

        def weight_grad(step, carry):
            for k in range(GROUP):
                place = kind * n + step * GROUP + k
                i = order[place]
                product = lax.dot_general(
                    x_ref[:, panel(row_of[i])], gp_ref[col_of[i]],
                    (((0,), (0,)), ((), ())), preferred_element_type=jnp.float32,
                )
                start = 0
                for p, rows in enumerate(ROWS):
                    first, second = (other_x, other_z) if X_FIRST[p] else (other_z, other_x)
                    outs[2 * p + first][second * n + step * GROUP + k] = product[start:start + rows]
                    start += rows
            return carry

        lax.fori_loop(0, n // GROUP, weight_grad, 0)
    for copy in leaving:
        copy.wait()


def along_z(value, sizes, move):
    n_dp, n_tensor = sizes
    z_len = n_dp // X_LO
    pairs = []
    for dp in range(n_dp):
        for tp in range(n_tensor):
            z = move(dp % z_len, tp % CORES) % z_len
            pairs.append((dp * n_tensor + tp, (dp - dp % z_len + z) * n_tensor + tp))
    return lax.ppermute(value, ("dp", "tensor"), pairs)


def partner(stride):
    return lambda z, core: z + stride * (1 - 2 * ((z // stride + core) % 2))


def swap_x(value, sizes):
    n_dp = sizes[0]
    return lax.ppermute(value, "dp", [(i, (i + n_dp // X_LO) % n_dp) for i in range(n_dp)])


def pick(value, at, count):
    return lax.dynamic_slice_in_dim(value, at * count, count, 0)


def swap_cores(value, sizes):
    return lax.ppermute(value, "tensor", [(i, i ^ 1) for i in range(sizes[1])])


def sum_over(value, axis, sizes):
    y_len = sizes[1] // (X_HI * CORES)
    index = lambda x, y, c: (x * y_len + y) * CORES + c
    if axis == "y":
        groups = [[index(x, y, c) for y in range(y_len)] for x in range(X_HI) for c in range(CORES)]
    else:
        groups = [[index(x, y, c) for x in range(X_HI)] for y in range(y_len) for c in range(CORES)]
    return lax.psum_scatter(value, "tensor", scatter_dimension=0, axis_index_groups=groups, tiled=True)


def reduce_all(parts, send, keep, sizes):
    z = lax.rem(lax.axis_index("dp"), sizes[0] // X_LO)
    core = lax.rem(lax.axis_index("tensor"), CORES)
    pair_z = lambda value: along_z(value, sizes, partner(1))
    pair_x = lambda value: swap_x(value, sizes)
    got_parts = [(pair_x if x_first else pair_z)(away) for (away, _), x_first in zip(parts, X_FIRST)]
    panels = sum_over(swap_cores(send, sizes) + keep, "y", sizes)
    sums = []
    for got, (_, here), x_first in zip(got_parts, parts, X_FIRST):
        n = got.shape[0] // 2
        sums.append(got[:n] + here[:n] + (pair_z if x_first else pair_x)(got[n:] + here[n:]))
    sums = [jnp.concatenate([sums[p] for p in group], axis=1) for group in GROUPED]
    stride = 2
    while sums[0].shape[0] > RING:
        half, digit = sums[0].shape[0] // 2, lax.rem(lax.div(z, stride), 2)
        if half == RING:
            sums[-1], panels = lax.optimization_barrier((sums[-1], panels))
            panels = sum_over(panels, "x_hi", sizes)
        sums = [
            pick(now, digit, half) + along_z(pick(now, 1 - digit, half), sizes, partner(stride)) for now in sums
        ]
        stride *= 2
    now = jnp.concatenate(sums, axis=1)
    panels = jnp.concatenate([panels[j] for j in range(panels.shape[0])], axis=1)
    mine, way = lax.div(z, stride), 1 - 2 * core
    chunk = lambda k: pick(now, lax.rem(mine + k * way + RING, RING), 1)
    near, total = None, chunk(0)
    far_way = lambda z, core: z + stride * (1 - 2 * core)
    opposite = lax.rem(mine + RING // 2, RING)
    far = jnp.concatenate([along_z(pick(part, opposite, 1), sizes, far_way) for part in sums], axis=1)
    for k in range(RING // 2, 0, -1):
        if near is not None:
            far, near = lax.optimization_barrier((far, near))
            near = along_z(near, sizes, lambda z, core: z - stride * (1 - 2 * core))
        if k < RING // 2:
            far = along_z(far, sizes, far_way)
        if k > 1:
            far = far + chunk(k - 1)
            near = chunk(1 - k) if near is None else near + chunk(1 - k)
    far, near, panels = lax.optimization_barrier((far, near, panels))
    return panels, total + far + near


def on_device(n_dp, n_tensor, activations, grad_hidden, weight_tiles, tile_slots, owner_map):
    tok_rows, width = activations.shape
    n_tiles = tile_slots.shape[1]
    n_cols = grad_hidden.shape[1] // TILE
    row_panels = width // TILE
    per = row_panels // n_tensor
    z_len = n_dp // X_LO
    y_len = n_tensor // (X_HI * CORES)
    hbm = pl.BlockSpec(memory_space=pl.ANY)
    vmem = pl.BlockSpec(memory_space=pltpu.VMEM)
    flops = 2 * n_tiles * tok_rows * TILE * TILE
    f32 = lambda *shape: jax.ShapeDtypeStruct(shape, jnp.float32)
    f32_parts = [f32(n_tiles // 2, rows, TILE) for rows in ROWS for _ in range(2)]
    send, keep, *parts = pl.pallas_call(
        functools.partial(tile_kernel, n_tiles, n_cols, per, z_len, y_len),
        out_shape=(f32(row_panels // 2, tok_rows, TILE), f32(row_panels // 2, tok_rows, TILE), *f32_parts),
        in_specs=[hbm] * 5,
        out_specs=(hbm, hbm) + (vmem,) * len(f32_parts),
        scratch_shapes=[
            pltpu.VMEM(activations.shape, jnp.bfloat16),
            pltpu.VMEM(grad_hidden.shape, jnp.bfloat16),
            pltpu.VMEM((n_tiles, TILE, TILE), jnp.bfloat16),
            pltpu.VMEM((n_cols, tok_rows, TILE), jnp.float32),
            pltpu.VMEM((n_cols, tok_rows, TILE), jnp.bfloat16),
            pltpu.VMEM((row_panels, tok_rows, TILE), jnp.float32),
            pltpu.SMEM((1, n_tiles), jnp.int32),
            pltpu.SMEM((1, n_tiles), jnp.int32),
            *[pltpu.SMEM((n_tiles,), jnp.int32)] * 3,
            pltpu.SemaphoreType.DMA((6 + TILE_COPIES,)),
        ],
        compiler_params=pltpu.CompilerParams(vmem_limit_bytes=VMEM_LIMIT),
        cost_estimate=pl.CostEstimate(flops=3 * flops, bytes_accessed=12 * 2**20, transcendentals=0),
    )(tile_slots, owner_map, activations, grad_hidden, weight_tiles[0])
    pairs = [(parts[2 * p + 1], parts[2 * p]) for p in range(len(ROWS))]
    return reduce_all(pairs, send, keep, (n_dp, n_tensor))


def solution(mesh):
    return jax.shard_map(
        functools.partial(on_device, mesh.shape["dp"], mesh.shape["tensor"]),
        mesh=mesh,
        in_specs=(
            P("dp", None),
            P("dp", "tensor"),
            P("tensor", None, None, None),
            P("tensor", None),
            P("tensor", None),
        ),
        out_specs=(P("dp", "tensor"), P("dp", "tensor", None)),
        check_vma=False,
    )
```
